32 devices in a mesh: groups: 1, dom: 4 (over z), cls: 4 (over y, x), pix: 2 (over core).
Axes of the slice: x: 2, y: 2, z: 4, core: 2. Of those that a mesh axis runs over, the one named last changes fastest.
Arguments:
- particles: float32 [512, 2, 4096], P(('groups', 'dom', 'cls', 'pix')), may hold values from -10 to 10
- templates: bfloat16 [100, 2, 4096], P(('groups', 'cls')), may hold values from -0.5 to 0.5
- offsets: int32 [9, 2], replicated, may hold values from -3 to 3, as said below
- micrograph: int32 [512], P(('groups', 'dom', 'cls', 'pix')), may hold values from 0 to 63
- noise_var: float32 [64], P('groups'), may hold values from 0.25 to 2
- prior_rot: int32 [512], P(('groups', 'dom', 'cls', 'pix')), may hold values from 0 to 3
- earlier_class_labels: int32 [512], P(('groups', 'dom', 'cls', 'pix')), may hold values from 0 to 99
Outputs:
- class_sums: float32 [100, 2, 4096], P(('groups', 'cls'), None, ('dom', 'pix'))
- class_weights: float32 [100], P(('groups', 'cls'))
- log_evidence: float32 [1], P('groups')
The draws below stay inside these ranges and needn't reach their ends.
Inputs may be any that keep to these rules, and one draw needn't show every extreme that they name: 9 distinct offsets on the 7 x 7 grid of whole-pixel shifts, with (-3, -3) and (3, 3) among them.
All inputs are finite; a program needn't handle non-finite values.
Results may differ from the reference program's by a relative error of at most 0.008.
Values may be sent and summed in bfloat16 or wider, within the bound.
A program may use at most 192 MiB of HBM per device.

```python
import math
import jax
import jax.numpy as jnp
from jax import lax

RAD = 32
ANG = 128
CLASS_COUNT = 100
ROT = 4
NT = 9
NM = 64
PART_DEV = 16
PARTICLES = 512


def class_images(key):
    template_base = 0.06 * jnp.clip(jax.random.normal(jax.random.fold_in(key, 11), (CLASS_COUNT, 2, RAD, ANG), jnp.float32), -4.0, 4.0)
    return template_base


def draw_templates(key, part):
    return class_images(key).reshape(CLASS_COUNT, 2, RAD * ANG).astype(jnp.bfloat16)


def draw_particles(key, part):
    template_base = class_images(key)
    labels = jax.random.randint(jax.random.fold_in(key, 13), (PARTICLES,), 0, CLASS_COUNT)
    turn_draw = jax.random.randint(jax.random.fold_in(key, 14), (PARTICLES,), 0, ROT)
    angle_index = (jnp.arange(ANG, dtype=jnp.int32)[None, :] - turn_draw[:, None] * (ANG // ROT)) % ANG
    chosen = template_base[labels]
    angle_index = jnp.broadcast_to(angle_index[:, None, None, :], chosen.shape)
    rotated = jnp.take_along_axis(chosen, angle_index, axis=3)
    amplitude = 1.5
    noise_part = jnp.clip(jax.random.normal(jax.random.fold_in(key, 16), chosen.shape, jnp.float32), -4.0, 4.0)
    return (amplitude * rotated + noise_part).reshape(PARTICLES, 2, RAD * ANG).astype(jnp.float32)


def draw_offsets(key, part):
    chosen_cells = jax.random.permutation(jax.random.fold_in(key, 21), 47)[:NT - 2] + 1
    grid_cells = jnp.concatenate([jnp.array([0, 48], jnp.int32), chosen_cells.astype(jnp.int32)])
    return jnp.stack([grid_cells // 7 - 3, grid_cells % 7 - 3], axis=1).astype(jnp.int32)


def with_ends(values, rng, smallest, top_value):
    index_at = [jax.random.randint(jax.random.fold_in(rng, axis), (), 0, length) for axis, length in enumerate(values.shape)]
    longest = values.shape.index(max(values.shape))
    beside = index_at[:longest] + [(index_at[longest] + 1) % values.shape[longest]] + index_at[longest + 1:]
    return values.at[tuple(index_at)].set(smallest).at[tuple(beside)].set(top_value)


def setup_inputs(seed: int = 0, part: int = 0) -> dict:
    arg_keys = jax.random.split(jax.random.key(seed), 8)
    own_keys = jax.random.split(jax.random.fold_in(arg_keys[7], part), 8)
    particles = draw_particles(jax.random.fold_in(jax.random.fold_in(arg_keys[7], part), 71), part)
    templates = draw_templates(jax.random.fold_in(jax.random.fold_in(arg_keys[7], part), 71), part)
    offsets = draw_offsets(jax.random.fold_in(arg_keys[7], 71), part)
    micrograph = with_ends(jax.random.randint(own_keys[3], (PARTICLES,), 0, NM), jax.random.fold_in(own_keys[3], 1), 0, NM - 1).astype(jnp.int32)
    noise_var = jnp.clip(jnp.exp(jax.random.uniform(own_keys[4], (NM,), jnp.float32, math.log(0.25), math.log(2.0))), 0.25, 2.0)
    prior_rot = with_ends(jax.random.randint(own_keys[5], (PARTICLES,), 0, ROT), jax.random.fold_in(own_keys[5], 1), 0, ROT - 1).astype(jnp.int32)
    earlier_class_labels = with_ends(jax.random.randint(own_keys[6], (PARTICLES,), 0, CLASS_COUNT), jax.random.fold_in(own_keys[6], 1), 0, CLASS_COUNT - 1).astype(jnp.int32)
    return {"particles": particles, "templates": templates, "offsets": offsets, "micrograph": micrograph, "noise_var": noise_var, "prior_rot": prior_rot, "earlier_class_labels": earlier_class_labels}


KAPPA = 2.0
PRIOR_REWARD = 1.5
MOVE_WEIGHT = 0.125


def shifted_images(particles, offsets):
    radius = jnp.arange(RAD, dtype=jnp.float32) + 1.0
    angle_grid = (2.0 * math.pi / ANG) * jnp.arange(ANG, dtype=jnp.float32)
    wave_first = (radius[:, None] * jnp.cos(angle_grid)[None, :]).reshape(-1)
    wave_second = (radius[:, None] * jnp.sin(angle_grid)[None, :]).reshape(-1)
    offset_first = offsets[:, 0].astype(jnp.float32)
    offset_second = offsets[:, 1].astype(jnp.float32)
    phase_table = (2.0 * math.pi / (2 * RAD)) * (offset_first[:, None] * wave_first[None, :] + offset_second[:, None] * wave_second[None, :])
    cosine = jnp.cos(phase_table)[None]
    sine_part = jnp.sin(phase_table)[None]
    real_part = particles[:, 0, :][:, None, :]
    imag_part = particles[:, 1, :][:, None, :]
    new_real = real_part * cosine + imag_part * sine_part
    new_imag = imag_part * cosine - real_part * sine_part
    return jnp.stack([new_real, new_imag], axis=2).astype(jnp.bfloat16)


def row_terms(micrograph, prior_rot, earlier_class_labels, noise_var, offsets):
    inverse = jnp.sum(jnp.where(micrograph[:, None] == jnp.arange(noise_var.shape[0], dtype=jnp.int32)[None, :], 1.0 / noise_var[None, :], 0.0), axis=1)
    turn_prior = KAPPA * jnp.cos((2.0 * math.pi / ROT) * (jnp.arange(ROT, dtype=jnp.int32)[:, None] - prior_rot[None, :]).astype(jnp.float32))
    class_agreement = jnp.where(jnp.arange(CLASS_COUNT, dtype=jnp.int32)[:, None] == earlier_class_labels[None, :], PRIOR_REWARD, 0.0)
    offset_first = offsets[:, 0].astype(jnp.float32)
    offset_second = offsets[:, 1].astype(jnp.float32)
    move_prior = -MOVE_WEIGHT * (offset_first * offset_first + offset_second * offset_second)
    return inverse, turn_prior, class_agreement, move_prior


def reference(particles, templates, offsets, micrograph, noise_var, prior_rot, earlier_class_labels):
    step_size = ANG // ROT
    feature_count = RAD * ANG
    particle_total = particles.shape[0]
    shift_count = offsets.shape[0]
    rotation_index = (jnp.arange(ANG, dtype=jnp.int32)[None, :] - step_size * jnp.arange(ROT, dtype=jnp.int32)[:, None]) % ANG
    polar_grid = templates.reshape(CLASS_COUNT, 2, RAD, ANG)
    rotated = jnp.take(polar_grid, rotation_index, axis=3)
    rotated = jnp.transpose(rotated, (3, 0, 1, 2, 4)).reshape(ROT * CLASS_COUNT, 2 * feature_count)
    widened = templates.astype(jnp.float32)
    energy = jnp.sum(widened * widened, axis=(1, 2))
    inverse, turn_prior, class_agreement, move_prior = row_terms(micrograph, prior_rot, earlier_class_labels, noise_var, offsets)
    batch_size = PART_DEV
    batch_count = particle_total // batch_size
    batches = (
        particles.reshape(batch_count, batch_size, 2, feature_count),
        inverse.reshape(batch_count, batch_size),
        jnp.transpose(turn_prior.reshape(ROT, batch_count, batch_size), (1, 0, 2)),
        jnp.transpose(class_agreement.reshape(CLASS_COUNT, batch_count, batch_size), (1, 0, 2)),
    )

    def batch_step(loop_state, batch_data):
        aligned_sum, weight_sum, evidence_sum = loop_state
        batch_particles, batch_inverse, batch_turn, batch_match = batch_data
        images_flat = shifted_images(batch_particles, offsets).reshape(batch_size * shift_count, 2 * feature_count)
        correlation = jnp.dot(rotated, images_flat.T, preferred_element_type=jnp.float32).reshape(ROT, CLASS_COUNT, batch_size, shift_count)
        values = (correlation - 0.5 * energy[None, :, None, None]) * batch_inverse[None, None, :, None] + move_prior[None, None, None, :] + batch_turn[:, None, :, None] + batch_match[None, :, :, None]
        highest = jnp.max(values, axis=(0, 1, 3))
        evidence = highest + jnp.log(jnp.sum(jnp.exp(values - highest[None, None, :, None]), axis=(0, 1, 3)))
        posterior = jnp.exp(values - evidence[None, None, :, None]).astype(jnp.bfloat16)
        weight_sum = weight_sum + jnp.sum(posterior.astype(jnp.float32), axis=(0, 2, 3))
        aligned_sum = aligned_sum + jnp.dot(posterior.reshape(ROT * CLASS_COUNT, batch_size * shift_count), images_flat, preferred_element_type=jnp.float32)
        return (aligned_sum, weight_sum, evidence_sum + jnp.sum(evidence)), None

    initial = (jnp.zeros((ROT * CLASS_COUNT, 2 * feature_count), jnp.float32), jnp.zeros((CLASS_COUNT,), jnp.float32), jnp.zeros((), jnp.float32))
    final_state, unused = lax.scan(batch_step, initial, batches)
    aligned_sum, weight_sum, evidence_sum = final_state
    aligned = aligned_sum.reshape(ROT, CLASS_COUNT, 2, RAD, ANG)
    undo_index = (jnp.arange(ANG, dtype=jnp.int32)[None, :] + step_size * jnp.arange(ROT, dtype=jnp.int32)[:, None]) % ANG
    class_sums = jnp.zeros((CLASS_COUNT, 2, RAD, ANG), jnp.float32)
    for rotation in range(ROT):
        class_sums = class_sums + jnp.take(aligned[rotation], undo_index[rotation], axis=3)
    log_evidence = (evidence_sum / particle_total)[None]
    return class_sums.reshape(CLASS_COUNT, 2, feature_count), weight_sum, log_evidence
```

```python
import functools
import math

import jax
import jax.numpy as jnp
import numpy as np
from jax import lax
from jax.experimental import pallas as pl
from jax.experimental.pallas import tpu as pltpu
from jax.sharding import PartitionSpec as P

RAD = 32
ANG = 128
CLASS_COUNT = 100
ROT = 4


KAPPA = 2.0
PRIOR_REWARD = 1.5
MOVE_WEIGHT = 0.125


def shifted_images(particles, offsets):
    radius = jnp.arange(RAD, dtype=jnp.float32) + 1.0
    angle_grid = 2.0 * math.pi / ANG * jnp.arange(ANG, dtype=jnp.float32)
    wave_first = (radius[:, None] * jnp.cos(angle_grid)[None, :]).reshape(-1)
    wave_second = (radius[:, None] * jnp.sin(angle_grid)[None, :]).reshape(-1)
    offset_first = offsets[:, 0].astype(jnp.float32)
    offset_second = offsets[:, 1].astype(jnp.float32)
    phase_table = (
        2.0
        * math.pi
        / (2 * RAD)
        * (
            offset_first[:, None] * wave_first[None, :]
            + offset_second[:, None] * wave_second[None, :]
        )
    )
    cosine = jnp.cos(phase_table)[None]
    sine_part = jnp.sin(phase_table)[None]
    real_part = particles[:, 0, :][:, None, :]
    imag_part = particles[:, 1, :][:, None, :]
    new_real = real_part * cosine + imag_part * sine_part
    new_imag = imag_part * cosine - real_part * sine_part
    return jnp.stack([new_real, new_imag], axis=2).astype(jnp.bfloat16)


def row_terms(micrograph, prior_rot, earlier_class_labels, noise_var, offsets):
    inverse = jnp.sum(
        jnp.where(
            micrograph[:, None] == jnp.arange(noise_var.shape[0], dtype=jnp.int32)[None, :],
            1.0 / noise_var[None, :],
            0.0,
        ),
        axis=1,
    )
    turn_prior = KAPPA * jnp.cos(
        2.0
        * math.pi
        / ROT
        * (jnp.arange(ROT, dtype=jnp.int32)[:, None] - prior_rot[None, :]).astype(jnp.float32)
    )
    class_agreement = jnp.where(
        jnp.arange(CLASS_COUNT, dtype=jnp.int32)[:, None] == earlier_class_labels[None, :],
        PRIOR_REWARD,
        0.0,
    )
    offset_first = offsets[:, 0].astype(jnp.float32)
    offset_second = offsets[:, 1].astype(jnp.float32)
    move_prior = -MOVE_WEIGHT * (offset_first * offset_first + offset_second * offset_second)
    return (inverse, turn_prior, class_agreement, move_prior)


def rotate_block(block_tmpl, first_rot, group_size):
    size_block = block_tmpl.shape[0]
    polar_grid = block_tmpl.reshape(size_block, 2, RAD, ANG)
    doubled = jnp.concatenate([polar_grid, polar_grid], axis=3)
    step_size = ANG // ROT
    pieces = [
        lax.dynamic_slice_in_dim(doubled, ANG - (first_rot + within) * step_size, ANG, 3)
        for within in range(group_size)
    ]
    return jnp.stack(pieces, axis=0).reshape(group_size * size_block, 2 * RAD * ANG)


def block_energy(block_tmpl):
    widened = block_tmpl.astype(jnp.float32)
    return jnp.sum(widened * widened, axis=(1, 2))


def split_features(sum_store):
    return lax.psum_scatter(sum_store, ("dom", "pix"), scatter_dimension=2, tiled=True)


def body(particles, templates, offsets, micrograph, noise_var, prior_rot, earlier_class_labels):
    particle_count = particles.shape[0]
    size_block = templates.shape[0]
    shift_count = offsets.shape[0]
    cls_size = lax.axis_size("cls")
    cls_index = lax.axis_index("cls")
    total_particles = particle_count * lax.axis_size("dom") * cls_size * lax.axis_size("pix")
    group_size = math.gcd(ROT, 4)
    group_count = ROT // group_size
    step_size = ANG // ROT
    feature_count = RAD * ANG
    kept_shape = (group_count, group_size, size_block, particle_count, shift_count)

    def scores(block_tmpl, energy, first_class, first_rot, images_flat, row_extras):
        inverse, turn_prior, class_agreement, move_prior = row_extras
        rotated = rotate_block(block_tmpl, first_rot, group_size)
        correlation = lax.dot_general(
            rotated, images_flat, (((1,), (1,)), ((), ())), preferred_element_type=jnp.float32
        )
        correlation = correlation.reshape(group_size, size_block, particle_count, shift_count)
        match_part = lax.dynamic_slice_in_dim(class_agreement, first_class, size_block, 0)
        return (
            (correlation - 0.5 * energy[None, :, None, None]) * inverse[None, None, :, None]
            + move_prior[None, None, None, :]
            + turn_prior[:, None, :, None]
            + match_part[None, :, :, None]
        )

    def normalize_block(block_tmpl, first_class, images_flat, row_extras, loop_state):
        energy = block_energy(block_tmpl)

        def normalize_group_turn(group_index, inner_state):
            highest, running_sum, kept = inner_state
            values = scores(
                block_tmpl, energy, first_class, group_index * group_size, images_flat, row_extras
            )
            new_high = jnp.maximum(highest, jnp.max(values, axis=(0, 1, 3)))
            running_sum = running_sum * jnp.exp(highest - new_high) + jnp.sum(
                jnp.exp(values - new_high[None, None, :, None]), axis=(0, 1, 3)
            )
            kept = lax.dynamic_update_index_in_dim(kept, values, group_index, 0)
            return (new_high, running_sum, kept)

        initial = (loop_state[0], loop_state[1], jnp.zeros(kept_shape, jnp.float32))
        return lax.fori_loop(0, group_count, normalize_group_turn, initial)

    def collect_block(kept, images_flat, evidence):

        def collect_group_turn(group_index, inner_state):
            block_sum, block_weight = inner_state
            first_rot = group_index * group_size
            values = lax.dynamic_index_in_dim(kept, group_index, 0, keepdims=False)
            posterior = jnp.exp(values - evidence[None, None, :, None]).astype(jnp.bfloat16)
            block_weight = block_weight + jnp.sum(posterior.astype(jnp.float32), axis=(0, 2, 3))
            aligned = jnp.dot(
                posterior.reshape(group_size * size_block, particle_count * shift_count),
                images_flat,
                preferred_element_type=jnp.float32,
            )
            aligned = aligned.reshape(group_size, size_block, 2, RAD, ANG)
            doubled = jnp.concatenate([aligned, aligned], axis=4)
            for within in range(group_size):
                block_sum = block_sum + lax.dynamic_slice_in_dim(
                    doubled[within], (first_rot + within) * step_size, ANG, 3
                )
            return (block_sum, block_weight)

        initial = (
            jnp.zeros((size_block, 2, RAD, ANG), jnp.float32),
            jnp.zeros((size_block,), jnp.float32),
        )
        block_sum, block_weight = lax.fori_loop(0, group_count, collect_group_turn, initial)
        return (block_sum.reshape(size_block, 2, feature_count), block_weight)

    own_first = cls_index * size_block
    all_kept = jnp.zeros((cls_size,) + kept_shape, jnp.float32)
    prepare_images_flat = shifted_images(particles, offsets).reshape(
        particles.shape[0] * shift_count, 2 * feature_count
    )
    prepare_row_extras = row_terms(micrograph, prior_rot, earlier_class_labels, noise_var, offsets)
    images_flat = prepare_images_flat
    row_extras = prepare_row_extras
    held_block = lax.all_gather(templates, "cls", axis=0, tiled=True)

    def current_block(held_now, owner_index):
        return lax.dynamic_slice_in_dim(held_now, owner_index * size_block, size_block, 0)

    def first_turn(turn_index, outer_state):
        held_now, highest, running_sum, retained_entries = outer_state
        owner_index = (cls_index - turn_index) % cls_size
        highest, running_sum, kept = normalize_block(
            current_block(held_now, owner_index),
            owner_index * size_block,
            images_flat,
            row_extras,
            (highest, running_sum),
        )
        retained_entries = lax.dynamic_update_index_in_dim(retained_entries, kept, turn_index, 0)
        return (held_now, highest, running_sum, retained_entries)

    highest, running_sum = (
        jnp.full((particle_count,), -jnp.inf, jnp.float32),
        jnp.zeros((particle_count,), jnp.float32),
    )
    held_block, highest, running_sum, all_kept = lax.fori_loop(
        0, cls_size, first_turn, (held_block, highest, running_sum, all_kept)
    )
    evidence = highest + jnp.log(running_sum)

    def second_turn(turn_index, outer_state):
        sum_store, weights_all = outer_state
        owner_index = (cls_index - turn_index) % cls_size
        kept = lax.dynamic_index_in_dim(all_kept, turn_index, 0, keepdims=False)
        block_sum, block_weight = collect_block(kept, images_flat, evidence)
        weights_all = lax.dynamic_update_slice_in_dim(
            weights_all, block_weight, owner_index * size_block, 0
        )
        sum_store = lax.dynamic_update_slice_in_dim(
            sum_store, block_sum, owner_index * size_block, 0
        )
        return (sum_store, weights_all)

    store_rows = CLASS_COUNT
    initial = (
        jnp.zeros((store_rows, 2, feature_count), jnp.float32),
        jnp.zeros((CLASS_COUNT,), jnp.float32),
    )
    sum_store, weights_all = lax.fori_loop(0, cls_size, second_turn, initial)
    local_evidence = jnp.sum(evidence)
    sum_store = lax.psum_scatter(sum_store, "cls", scatter_dimension=0, tiled=True)
    class_sums = split_features(sum_store)
    weight_total, summed_evidence = lax.psum(
        (weights_all, local_evidence[None]), ("dom", "cls", "pix")
    )
    class_weights = lax.dynamic_slice_in_dim(weight_total, own_first, size_block, 0)
    log_evidence = summed_evidence / total_particles
    return (class_sums, class_weights, log_evidence)


AXES = ("groups", "dom", "cls", "pix")
PAD = 32


def wave_tables():
    radius = np.arange(RAD) + 1.0
    angle = 2.0 * np.pi / ANG * np.arange(ANG)
    first = (radius[:, None] * np.cos(angle)[None, :]).reshape(-1) * (2.0 * np.pi / (2 * RAD))
    second = (radius[:, None] * np.sin(angle)[None, :]).reshape(-1) * (2.0 * np.pi / (2 * RAD))
    rows = [np.cos(first), np.sin(first), np.cos(second), np.sin(second)]
    return np.stack(rows + rows).astype(np.float32)


def powers(cosine, sine_part, amount):
    c2, s2 = cosine * cosine - sine_part * sine_part, 2.0 * cosine * sine_part
    c3, s3 = c2 * cosine - s2 * sine_part, s2 * cosine + c2 * sine_part
    size = jnp.abs(amount)
    c = jnp.where(size < 0.5, 1.0, jnp.where(size < 1.5, cosine, jnp.where(size < 2.5, c2, c3)))
    s = jnp.where(size < 0.5, 0.0, jnp.where(size < 1.5, sine_part, jnp.where(size < 2.5, s2, s3)))
    return c, jnp.where(amount < 0.0, -s, s)


def fused(
    dims, part_ref, tmpl_ref, wave_ref, ext_ref, out_ref, small_ref,
    held, images, corr, total, sib_out, sib_in, cls_out, cls_in, dom_out, dom_in, small_in,
    own_sem, gather_s, gather_r, forward_s, forward_r, sib_s, sib_r, cls_s, cls_r,
    dom_s, dom_r, small_s, small_r, small_a, small_b, small_c,
):
    doms, clss, count, shifts, chunk = dims
    group, dom = lax.axis_index("groups"), lax.axis_index("dom")
    cls, pix = lax.axis_index("cls"), lax.axis_index("pix")
    other = 1 - pix
    sibling = (group, dom, cls, other)
    cls_peers = [(group, dom, lax.rem(cls + k, clss), pix) for k in range(1, clss)]
    dom_peers = [(group, lax.rem(dom + k, doms), cls, pix) for k in range(1, doms)]
    mesh_id = pl.DeviceIdType.MESH

    def send(src, dst, s, r, target):
        copy = pltpu.make_async_remote_copy(
            src_ref=src, dst_ref=dst, send_sem=s, recv_sem=r,
            device_id=target, device_id_type=mesh_id,
        )
        copy.start()
        return copy

    barrier = pltpu.get_barrier_semaphore()
    for target in [sibling] + cls_peers + dom_peers:
        pl.semaphore_signal(barrier, inc=1, device_id=target, device_id_type=mesh_id)
    pl.semaphore_wait(barrier, clss + doms - 1)

    pending = []
    gathers = [
        send(tmpl_ref.at[pix], held.at[pix, cls], gather_s.at[k], gather_r.at[k], target)
        for k, target in enumerate(cls_peers)
    ]
    own_copies = [
        pltpu.make_async_copy(tmpl_ref.at[c], held.at[c, cls], own_sem.at[c]) for c in range(2)
    ]
    for copy in own_copies:
        copy.start()

    step_size = ANG // ROT
    per_rot = shifts * count
    move_x = ext_ref[:, 40:41] + jnp.zeros((count, ANG), jnp.float32)
    move_y = ext_ref[:, 41:42] + jnp.zeros((count, ANG), jnp.float32)

    def make_images(g, carry):
        lanes = pl.ds(pl.multiple_of(g * ANG, ANG), ANG)
        waves = wave_ref[:, lanes]
        cx, sx = powers(waves[0:1], waves[1:2], move_x)
        cy, sy = powers(waves[2:3], waves[3:4], move_y)
        cosine = cx * cy - sx * sy
        sine_part = sx * cy + cx * sy
        real, imag = part_ref[0, :, lanes], part_ref[1, :, lanes]
        for rot in range(ROT):
            if rot:
                turn = ANG - rot * step_size
                co, si = pltpu.roll(cosine, turn, 1), pltpu.roll(sine_part, turn, 1)
                re, im = pltpu.roll(real, turn, 1), pltpu.roll(imag, turn, 1)
            else:
                co, si, re, im = cosine, sine_part, real, imag
            for t in range(shifts):
                c, s = co[t : t + 1], si[t : t + 1]
                row = rot * per_rot + t * count
                images[0, row : row + count, lanes] = (re * c + im * s).astype(jnp.bfloat16)
                images[1, row : row + count, lanes] = (im * c - re * s).astype(jnp.bfloat16)
        return carry

    lax.fori_loop(0, RAD, make_images, 0)

    forwards = []
    for k, copy in enumerate(gathers):
        copy.wait_recv()
        owner = lax.rem(cls + clss - 1 - k, clss)
        forwards.append(
            send(held.at[pix, owner], held.at[pix, owner], forward_s.at[k], forward_r.at[k], sibling)
        )
    for copy in own_copies:
        copy.wait()

    piece = 512
    corr[...] = jnp.zeros_like(corr)

    def correlate(comp):
        def step(n, energy):
            lanes = pl.ds(pl.multiple_of(n * piece, piece), piece)
            tmpl = held[comp, :, :, lanes].reshape(clss * PAD, piece)
            corr[...] += lax.dot_general(
                tmpl, images[comp, :, lanes], (((1,), (1,)), ((), ())),
                preferred_element_type=jnp.float32,
            )
            wide = tmpl.astype(jnp.float32)
            wide = wide * wide
            for q in range(piece // ANG):
                energy = energy + wide[:, q * ANG : (q + 1) * ANG]
            return energy
        return step

    energy = jnp.zeros((clss * PAD, ANG), jnp.float32)
    energy = lax.fori_loop(0, RAD * ANG // piece, correlate(pix), energy)
    for copy in forwards:
        copy.wait_recv()
    energy = lax.fori_loop(0, RAD * ANG // piece, correlate(other), energy)
    energy = jnp.sum(energy, axis=1, keepdims=True)

    turned = jnp.transpose(corr[...] - 0.5 * energy).reshape(ROT * shifts, count, clss * PAD)
    slot = lax.broadcasted_iota(jnp.int32, (count, clss * PAD), 1)
    inverse = ext_ref[:, 0:1]
    match = jnp.where(slot.astype(jnp.float32) == ext_ref[:, 1:2], PRIOR_REWARD, 0.0)
    real_class = lax.rem(slot, PAD) < CLASS_COUNT // clss
    match = jnp.where(real_class, match, -1e30)
    values = [
        turned[n] * inverse + (match + ext_ref[:, 2 + n : 3 + n]) for n in range(ROT * shifts)
    ]
    highest = functools.reduce(jnp.maximum, values)
    highest = jnp.max(highest, axis=1, keepdims=True)
    summed = functools.reduce(jnp.add, [jnp.exp(v - highest) for v in values])
    evidence = highest + jnp.log(jnp.sum(summed, axis=1, keepdims=True))
    posterior = [
        jnp.exp(v - evidence).astype(jnp.bfloat16).astype(jnp.float32) for v in values
    ]
    weights = jnp.sum(functools.reduce(jnp.add, posterior), axis=0, keepdims=True)
    evidence_row = jnp.sum(evidence + jnp.zeros((count, clss * PAD), jnp.float32), axis=0, keepdims=True)
    first_row = lax.broadcasted_iota(jnp.int32, (8, clss * PAD), 0) == 0
    small_a[...] = jnp.where(first_row, weights, evidence_row)
    small_sib = send(small_a, small_in.at[0], small_s.at[0], small_r.at[0], sibling)
    posterior = jnp.transpose(jnp.concatenate(posterior, axis=0)).astype(jnp.bfloat16)

    def block_dot(d, half, comp):
        lanes = pl.ds(pl.multiple_of((d * 2 + half) * chunk, chunk), chunk)
        return jnp.dot(
            posterior, images[comp, :, lanes], preferred_element_type=jnp.float32
        ).reshape(clss, PAD, chunk)

    order = [lax.rem(dom + j + 1, doms) for j in range(doms)]
    sib_copies, cls_copies = [], []

    def finish(j):
        sib_copies[j].wait_recv()
        for comp in range(2):
            value = total[j, :, comp] + sib_in[j, :, comp].astype(jnp.float32)
            total[j, :, comp] = value
            cls_out[j, :, comp] = value.astype(jnp.bfloat16)
        cls_copies.append([
            send(cls_out.at[j, lax.rem(cls + k + 1, clss)], cls_in.at[j, k],
                 cls_s.at[j, k], cls_r.at[j, k], target)
            for k, target in enumerate(cls_peers)
        ])

    for j in range(doms):
        for comp in range(2):
            sib_out[j, :, comp] = block_dot(order[j], other, comp).astype(jnp.bfloat16)
        sib_copies.append(send(sib_out.at[j], sib_in.at[j], sib_s.at[j], sib_r.at[j], sibling))
        if j:
            finish(j - 1)
        for comp in range(2):
            total[j, :, comp] = block_dot(order[j], pix, comp)
        if j == 0:
            small_sib.wait_recv()
            small_b[...] = small_a[...] + small_in[0]
            small_cls = [
                send(small_b, small_in.at[1 + k], small_s.at[1 + k], small_r.at[1 + k], target)
                for k, target in enumerate(cls_peers)
            ]
    finish(doms - 1)

    for copy in small_cls:
        copy.wait_recv()
    small_c[...] = functools.reduce(jnp.add, [small_b[...]] + [small_in[1 + k] for k in range(clss - 1)])
    small_dom = [
        send(small_c, small_in.at[clss + k], small_s.at[clss + k], small_r.at[clss + k], target)
        for k, target in enumerate(dom_peers)
    ]

    dom_copies = []
    for j in range(doms):
        for copy in cls_copies[j]:
            copy.wait_recv()
        value = total[j, cls]
        for k in range(clss - 1):
            value = value + cls_in[j, k].astype(jnp.float32)
        if j < doms - 1:
            dom_out[j] = value.astype(jnp.bfloat16)
            dom_copies.append(
                send(dom_out.at[j], dom_in.at[j], dom_s.at[j], dom_r.at[j], dom_peers[j])
            )
    for j in range(doms - 1):
        small_dom[j].wait_recv()
    small_ref[...] = functools.reduce(
        jnp.add, [small_c[...]] + [small_in[clss + k] for k in range(doms - 1)]
    )
    for j in range(doms - 1):
        dom_copies[j].wait_recv()
        value = value + dom_in[j].astype(jnp.float32)
    out_ref[...] = value
    for copy in gathers + forwards + sib_copies + sum(cls_copies, []) + dom_copies:
        copy.wait_send()
    for copy in [small_sib] + small_cls + small_dom:
        copy.wait_send()


def fused_body(doms, clss, particles, templates, offsets, micrograph, noise_var, prior_rot, earlier_class_labels):
    count, size_block, shifts = particles.shape[0], templates.shape[0], offsets.shape[0]
    chunk = RAD * ANG // (doms * 2)
    inverse, turn_prior, _, move_prior = row_terms(
        micrograph, prior_rot, earlier_class_labels, noise_var, offsets
    )
    slots = earlier_class_labels // size_block * PAD + earlier_class_labels % size_block
    bias = (turn_prior.T[:, :, None] + move_prior[None, None, :]).reshape(count, ROT * shifts)
    move = jnp.pad(offsets.astype(jnp.float32), ((0, count - shifts), (0, 0)))
    ext = jnp.concatenate(
        [inverse[:, None], slots.astype(jnp.float32)[:, None], bias,
         jnp.zeros((count, 38 - ROT * shifts), jnp.float32), move,
         jnp.zeros((count, ANG - 42), jnp.float32)], axis=1)
    tmpl = jnp.pad(jnp.transpose(templates, (1, 0, 2)), ((0, 0), (0, PAD - size_block), (0, 0)))
    part = jnp.transpose(particles, (1, 0, 2))
    rows = ROT * shifts * count
    bf, f32 = jnp.bfloat16, jnp.float32
    dma = pltpu.SemaphoreType.DMA
    vmem = pl.BlockSpec(memory_space=pltpu.VMEM)
    sums, small = pl.pallas_call(
        functools.partial(fused, (doms, clss, count, shifts, chunk)),
        out_shape=[
            jax.ShapeDtypeStruct((2, PAD, chunk), f32),
            jax.ShapeDtypeStruct((8, clss * PAD), f32),
        ],
        in_specs=[vmem] * 4,
        out_specs=[vmem] * 2,
        scratch_shapes=[
            pltpu.VMEM((2, clss, PAD, RAD * ANG), bf),
            pltpu.VMEM((2, rows, RAD * ANG), bf),
            pltpu.VMEM((clss * PAD, rows), f32),
            pltpu.VMEM((doms, clss, 2, PAD, chunk), f32),
            pltpu.VMEM((doms, clss, 2, PAD, chunk), bf),
            pltpu.VMEM((doms, clss, 2, PAD, chunk), bf),
            pltpu.VMEM((doms, clss, 2, PAD, chunk), bf),
            pltpu.VMEM((doms, clss - 1, 2, PAD, chunk), bf),
            pltpu.VMEM((doms - 1, 2, PAD, chunk), bf),
            pltpu.VMEM((doms - 1, 2, PAD, chunk), bf),
            pltpu.VMEM((clss + doms - 1, 8, clss * PAD), f32),
            dma((2,)), dma((clss - 1,)), dma((clss - 1,)), dma((clss - 1,)), dma((clss - 1,)),
            dma((doms,)), dma((doms,)), dma((doms, clss - 1)), dma((doms, clss - 1)),
            dma((doms - 1,)), dma((doms - 1,)), dma((clss + doms - 1,)), dma((clss + doms - 1,)),
            pltpu.VMEM((8, clss * PAD), f32),
            pltpu.VMEM((8, clss * PAD), f32),
            pltpu.VMEM((8, clss * PAD), f32),
        ],
        compiler_params=pltpu.CompilerParams(
            collective_id=0, has_side_effects=True, vmem_limit_bytes=44 * 2**20
        ),
    )(part, tmpl, jnp.asarray(wave_tables()), ext)
    class_sums = jnp.transpose(sums[:, :size_block], (1, 0, 2))
    class_weights = lax.dynamic_slice(small[0], (lax.axis_index("cls") * PAD,), (size_block,))
    log_evidence = small[1, :1] / (count * doms * clss * 2)
    return class_sums, class_weights, log_evidence


def solution(mesh):
    in_specs = (
        P(("groups", "dom", "cls", "pix"), None, None),
        P(("groups", "cls"), None, None),
        P(),
        P(("groups", "dom", "cls", "pix")),
        P("groups"),
        P(("groups", "dom", "cls", "pix")),
        P(("groups", "dom", "cls", "pix")),
    )
    out_specs = (P(("groups", "cls"), None, ("dom", "pix")), P(("groups", "cls")), P("groups"))
    doms, clss = mesh.shape["dom"], mesh.shape["cls"]
    whole_radii = RAD % (doms * mesh.shape["pix"]) == 0
    fits = mesh.shape["pix"] == 2 and doms > 1 and clss > 1 and clss * PAD <= ANG
    chosen = functools.partial(fused_body, doms, clss) if whole_radii and fits else body
    return jax.shard_map(chosen, mesh=mesh, in_specs=in_specs, out_specs=out_specs, check_vma=False)
```

```python
import functools
import math

import jax
import jax.numpy as jnp
import numpy as np
from jax import lax
from jax.experimental import pallas as pl
from jax.experimental.pallas import tpu as pltpu
from jax.sharding import PartitionSpec as P

RAD = 32
ANG = 128
CLASS_COUNT = 100
ROT = 4


KAPPA = 2.0
PRIOR_REWARD = 1.5
MOVE_WEIGHT = 0.125


def shifted_images(particles, offsets):
    radius = jnp.arange(RAD, dtype=jnp.float32) + 1.0
    angle_grid = 2.0 * math.pi / ANG * jnp.arange(ANG, dtype=jnp.float32)
    wave_first = (radius[:, None] * jnp.cos(angle_grid)[None, :]).reshape(-1)
    wave_second = (radius[:, None] * jnp.sin(angle_grid)[None, :]).reshape(-1)
    offset_first = offsets[:, 0].astype(jnp.float32)
    offset_second = offsets[:, 1].astype(jnp.float32)
    phase_table = (
        2.0
        * math.pi
        / (2 * RAD)
        * (
            offset_first[:, None] * wave_first[None, :]
            + offset_second[:, None] * wave_second[None, :]
        )
    )
    cosine = jnp.cos(phase_table)[None]
    sine_part = jnp.sin(phase_table)[None]
    real_part = particles[:, 0, :][:, None, :]
    imag_part = particles[:, 1, :][:, None, :]
    new_real = real_part * cosine + imag_part * sine_part
    new_imag = imag_part * cosine - real_part * sine_part
    return jnp.stack([new_real, new_imag], axis=2).astype(jnp.bfloat16)


def row_terms(micrograph, prior_rot, earlier_class_labels, noise_var, offsets):
    inverse = jnp.sum(
        jnp.where(
            micrograph[:, None] == jnp.arange(noise_var.shape[0], dtype=jnp.int32)[None, :],
            1.0 / noise_var[None, :],
            0.0,
        ),
        axis=1,
    )
    turn_prior = KAPPA * jnp.cos(
        2.0
        * math.pi
        / ROT
        * (jnp.arange(ROT, dtype=jnp.int32)[:, None] - prior_rot[None, :]).astype(jnp.float32)
    )
    class_agreement = jnp.where(
        jnp.arange(CLASS_COUNT, dtype=jnp.int32)[:, None] == earlier_class_labels[None, :],
        PRIOR_REWARD,
        0.0,
    )
    offset_first = offsets[:, 0].astype(jnp.float32)
    offset_second = offsets[:, 1].astype(jnp.float32)
    move_prior = -MOVE_WEIGHT * (offset_first * offset_first + offset_second * offset_second)
    return (inverse, turn_prior, class_agreement, move_prior)


def rotate_block(block_tmpl, first_rot, group_size):
    size_block = block_tmpl.shape[0]
    polar_grid = block_tmpl.reshape(size_block, 2, RAD, ANG)
    doubled = jnp.concatenate([polar_grid, polar_grid], axis=3)
    step_size = ANG // ROT
    pieces = [
        lax.dynamic_slice_in_dim(doubled, ANG - (first_rot + within) * step_size, ANG, 3)
        for within in range(group_size)
    ]
    return jnp.stack(pieces, axis=0).reshape(group_size * size_block, 2 * RAD * ANG)


def block_energy(block_tmpl):
    widened = block_tmpl.astype(jnp.float32)
    return jnp.sum(widened * widened, axis=(1, 2))


def split_features(sum_store):
    return lax.psum_scatter(sum_store, ("dom", "pix"), scatter_dimension=2, tiled=True)


def body(particles, templates, offsets, micrograph, noise_var, prior_rot, earlier_class_labels):
    particle_count = particles.shape[0]
    size_block = templates.shape[0]
    shift_count = offsets.shape[0]
    cls_size = lax.axis_size("cls")
    cls_index = lax.axis_index("cls")
    total_particles = particle_count * lax.axis_size("dom") * cls_size * lax.axis_size("pix")
    group_size = math.gcd(ROT, 4)
    group_count = ROT // group_size
    step_size = ANG // ROT
    feature_count = RAD * ANG
    kept_shape = (group_count, group_size, size_block, particle_count, shift_count)

    def scores(block_tmpl, energy, first_class, first_rot, images_flat, row_extras):
        inverse, turn_prior, class_agreement, move_prior = row_extras
        rotated = rotate_block(block_tmpl, first_rot, group_size)
        correlation = lax.dot_general(
            rotated, images_flat, (((1,), (1,)), ((), ())), preferred_element_type=jnp.float32
        )
        correlation = correlation.reshape(group_size, size_block, particle_count, shift_count)
        match_part = lax.dynamic_slice_in_dim(class_agreement, first_class, size_block, 0)
        return (
            (correlation - 0.5 * energy[None, :, None, None]) * inverse[None, None, :, None]
            + move_prior[None, None, None, :]
            + turn_prior[:, None, :, None]
            + match_part[None, :, :, None]
        )

    def normalize_block(block_tmpl, first_class, images_flat, row_extras, loop_state):
        energy = block_energy(block_tmpl)

        def normalize_group_turn(group_index, inner_state):
            highest, running_sum, kept = inner_state
            values = scores(
                block_tmpl, energy, first_class, group_index * group_size, images_flat, row_extras
            )
            new_high = jnp.maximum(highest, jnp.max(values, axis=(0, 1, 3)))
            running_sum = running_sum * jnp.exp(highest - new_high) + jnp.sum(
                jnp.exp(values - new_high[None, None, :, None]), axis=(0, 1, 3)
            )
            kept = lax.dynamic_update_index_in_dim(kept, values, group_index, 0)
            return (new_high, running_sum, kept)

        initial = (loop_state[0], loop_state[1], jnp.zeros(kept_shape, jnp.float32))
        return lax.fori_loop(0, group_count, normalize_group_turn, initial)

    def collect_block(kept, images_flat, evidence):

        def collect_group_turn(group_index, inner_state):
            block_sum, block_weight = inner_state
            first_rot = group_index * group_size
            values = lax.dynamic_index_in_dim(kept, group_index, 0, keepdims=False)
            posterior = jnp.exp(values - evidence[None, None, :, None]).astype(jnp.bfloat16)
            block_weight = block_weight + jnp.sum(posterior.astype(jnp.float32), axis=(0, 2, 3))
            aligned = jnp.dot(
                posterior.reshape(group_size * size_block, particle_count * shift_count),
                images_flat,
                preferred_element_type=jnp.float32,
            )
            aligned = aligned.reshape(group_size, size_block, 2, RAD, ANG)
            doubled = jnp.concatenate([aligned, aligned], axis=4)
            for within in range(group_size):
                block_sum = block_sum + lax.dynamic_slice_in_dim(
                    doubled[within], (first_rot + within) * step_size, ANG, 3
                )
            return (block_sum, block_weight)

        initial = (
            jnp.zeros((size_block, 2, RAD, ANG), jnp.float32),
            jnp.zeros((size_block,), jnp.float32),
        )
        block_sum, block_weight = lax.fori_loop(0, group_count, collect_group_turn, initial)
        return (block_sum.reshape(size_block, 2, feature_count), block_weight)

    own_first = cls_index * size_block
    all_kept = jnp.zeros((cls_size,) + kept_shape, jnp.float32)
    prepare_images_flat = shifted_images(particles, offsets).reshape(
        particles.shape[0] * shift_count, 2 * feature_count
    )
    prepare_row_extras = row_terms(micrograph, prior_rot, earlier_class_labels, noise_var, offsets)
    images_flat = prepare_images_flat
    row_extras = prepare_row_extras
    held_block = lax.all_gather(templates, "cls", axis=0, tiled=True)

    def current_block(held_now, owner_index):
        return lax.dynamic_slice_in_dim(held_now, owner_index * size_block, size_block, 0)

    def first_turn(turn_index, outer_state):
        held_now, highest, running_sum, retained_entries = outer_state
        owner_index = (cls_index - turn_index) % cls_size
        highest, running_sum, kept = normalize_block(
            current_block(held_now, owner_index),
            owner_index * size_block,
            images_flat,
            row_extras,
            (highest, running_sum),
        )
        retained_entries = lax.dynamic_update_index_in_dim(retained_entries, kept, turn_index, 0)
        return (held_now, highest, running_sum, retained_entries)

    highest, running_sum = (
        jnp.full((particle_count,), -jnp.inf, jnp.float32),
        jnp.zeros((particle_count,), jnp.float32),
    )
    held_block, highest, running_sum, all_kept = lax.fori_loop(
        0, cls_size, first_turn, (held_block, highest, running_sum, all_kept)
    )
    evidence = highest + jnp.log(running_sum)

    def second_turn(turn_index, outer_state):
        sum_store, weights_all = outer_state
        owner_index = (cls_index - turn_index) % cls_size
        kept = lax.dynamic_index_in_dim(all_kept, turn_index, 0, keepdims=False)
        block_sum, block_weight = collect_block(kept, images_flat, evidence)
        weights_all = lax.dynamic_update_slice_in_dim(
            weights_all, block_weight, owner_index * size_block, 0
        )
        sum_store = lax.dynamic_update_slice_in_dim(
            sum_store, block_sum, owner_index * size_block, 0
        )
        return (sum_store, weights_all)

    store_rows = CLASS_COUNT
    initial = (
        jnp.zeros((store_rows, 2, feature_count), jnp.float32),
        jnp.zeros((CLASS_COUNT,), jnp.float32),
    )
    sum_store, weights_all = lax.fori_loop(0, cls_size, second_turn, initial)
    local_evidence = jnp.sum(evidence)
    sum_store = lax.psum_scatter(sum_store, "cls", scatter_dimension=0, tiled=True)
    class_sums = split_features(sum_store)
    weight_total, summed_evidence = lax.psum(
        (weights_all, local_evidence[None]), ("dom", "cls", "pix")
    )
    class_weights = lax.dynamic_slice_in_dim(weight_total, own_first, size_block, 0)
    log_evidence = summed_evidence / total_particles
    return (class_sums, class_weights, log_evidence)


AXES = ("groups", "dom", "cls", "pix")
PAD = 32


def wave_tables():
    radius = np.arange(RAD) + 1.0
    angle = 2.0 * np.pi / ANG * np.arange(ANG)
    first = (radius[:, None] * np.cos(angle)[None, :]).reshape(-1) * (2.0 * np.pi / (2 * RAD))
    second = (radius[:, None] * np.sin(angle)[None, :]).reshape(-1) * (2.0 * np.pi / (2 * RAD))
    rows = [np.cos(first), np.sin(first), np.cos(second), np.sin(second)]
    return np.stack(rows + rows).astype(np.float32)


def powers(cosine, sine_part, amount):
    c2, s2 = cosine * cosine - sine_part * sine_part, 2.0 * cosine * sine_part
    c3, s3 = c2 * cosine - s2 * sine_part, s2 * cosine + c2 * sine_part
    size = jnp.abs(amount)
    c = jnp.where(size < 0.5, 1.0, jnp.where(size < 1.5, cosine, jnp.where(size < 2.5, c2, c3)))
    s = jnp.where(size < 0.5, 0.0, jnp.where(size < 1.5, sine_part, jnp.where(size < 2.5, s2, s3)))
    return c, jnp.where(amount < 0.0, -s, s)


def fused(
    dims, part_hbm, tmpl_ref, wave_ref, micro_ref, noise_ref, prior_ref, label_ref, move_ref,
    out_ref, weight_ref, evidence_ref, part_ref, held, images, corr, total, sib_out, sib_in, cls_out, cls_in, dom_out, dom_in, small_in,
    own_sem, part_sem, gather_s, gather_r, forward_s, forward_r, sib_s, sib_r, cls_s, cls_r,
    dom_s, dom_r, small_s, small_r, small_a, small_b, small_c, pair_s, pair_r,
):
    doms, clss, count, shifts, chunk = dims
    group, dom = lax.axis_index("groups"), lax.axis_index("dom")
    cls, pix = lax.axis_index("cls"), lax.axis_index("pix")
    other = 1 - pix
    sibling = (group, dom, cls, other)
    cls_peers = [(group, dom, lax.rem(cls + k, clss), pix) for k in range(1, clss)]
    dom_peers = [(group, lax.rem(dom + k, doms), cls, pix) for k in range(1, doms)]
    mesh_id = pl.DeviceIdType.MESH

    def send(src, dst, s, r, target):
        copy = pltpu.make_async_remote_copy(
            src_ref=src, dst_ref=dst, send_sem=s, recv_sem=r,
            device_id=target, device_id_type=mesh_id,
        )
        copy.start()
        return copy

    barrier = pltpu.get_barrier_semaphore()
    for target in [sibling] + cls_peers + dom_peers:
        pl.semaphore_signal(barrier, inc=1, device_id=target, device_id_type=mesh_id)
    pl.semaphore_wait(barrier, clss + doms - 1)

    odd = lax.rem(dom, 2)
    partner = (group, dom + 1 - 2 * odd, cls, pix)
    features = RAD * ANG
    part_size, common = 3 * features // 8, features // 4
    own_lanes = pl.ds(pl.multiple_of(odd * part_size, ANG), part_size)
    pair_lanes = pl.ds(pl.multiple_of((1 - odd) * part_size, ANG), part_size)
    common_lanes = pl.ds(2 * part_size, common)
    gathers = []
    for n, lanes in enumerate((own_lanes, common_lanes)):
        for k, target in enumerate(cls_peers):
            gathers.append(
                send(tmpl_ref.at[pix, :, lanes], held.at[pix, cls, :, lanes],
                     gather_s.at[n, k], gather_r.at[n, k], target)
            )
    own_copies = [
        pltpu.make_async_copy(tmpl_ref.at[c], held.at[c, cls], own_sem.at[c]) for c in range(2)
    ]
    part_copy = pltpu.make_async_copy(part_hbm, part_ref, part_sem)
    part_copy.start()
    for copy in own_copies:
        copy.start()

    rows = lax.broadcasted_iota(jnp.int32, (count, ANG), 0)
    noise = jnp.ones((count, ANG), jnp.float32)
    prior = jnp.zeros((count, ANG), jnp.int32)
    label = jnp.zeros((count, ANG), jnp.int32)
    for i in range(count):
        noise = jnp.where(rows == i, noise_ref[micro_ref[i]], noise)
        prior = jnp.where(rows == i, prior_ref[i], prior)
        label = jnp.where(rows == i, label_ref[i], label)
    move_x = jnp.zeros((count, ANG), jnp.int32)
    move_y = jnp.zeros((count, ANG), jnp.int32)
    for t in range(shifts):
        move_x = jnp.where(rows == t, move_ref[t, 0], move_x)
        move_y = jnp.where(rows == t, move_ref[t, 1], move_y)
    move_x, move_y = move_x.astype(jnp.float32), move_y.astype(jnp.float32)
    part_copy.wait()

    step_size = ANG // ROT
    per_rot = shifts * count

    def make_images(g, carry):
        lanes = pl.ds(pl.multiple_of(g * ANG, ANG), ANG)
        waves = wave_ref[:, lanes]
        cx, sx = powers(waves[0:1], waves[1:2], move_x)
        cy, sy = powers(waves[2:3], waves[3:4], move_y)
        cosine = cx * cy - sx * sy
        sine_part = sx * cy + cx * sy
        real, imag = part_ref[:, 0, lanes], part_ref[:, 1, lanes]
        for rot in range(ROT):
            if rot:
                turn = ANG - rot * step_size
                co, si = pltpu.roll(cosine, turn, 1), pltpu.roll(sine_part, turn, 1)
                re, im = pltpu.roll(real, turn, 1), pltpu.roll(imag, turn, 1)
            else:
                co, si, re, im = cosine, sine_part, real, imag
            for t in range(shifts):
                c, s = co[t : t + 1], si[t : t + 1]
                row = rot * per_rot + t * count
                images[0, row : row + count, lanes] = (re * c + im * s).astype(jnp.bfloat16)
                images[1, row : row + count, lanes] = (im * c - re * s).astype(jnp.bfloat16)
        return carry

    lax.fori_loop(0, RAD, make_images, 0)

    owners = [lax.rem(cls + clss - 1 - k, clss) for k in range(clss - 1)]
    forwards, pairs = [], []

    def forward(n, k, lanes):
        block = held.at[pix, owners[k], :, lanes]
        forwards.append(send(block, block, forward_s.at[n, k], forward_r.at[n, k], sibling))

    for k in range(clss - 1):
        gathers[k].wait_recv()
        block = held.at[pix, owners[k], :, own_lanes]
        pairs.append(send(block, block, pair_s.at[k], pair_r.at[k], partner))
        forward(0, k, own_lanes)
    for k in range(clss - 1):
        gathers[clss - 1 + k].wait_recv()
        forward(1, k, common_lanes)
    for k in range(clss - 1):
        pairs[k].wait_recv()
        forward(2, k, pair_lanes)
    for copy in own_copies:
        copy.wait()

    piece = 512
    corr[...] = jnp.zeros_like(corr)

    def correlate(comp):
        def step(n, energy):
            lanes = pl.ds(pl.multiple_of(n * piece, piece), piece)
            tmpl = held[comp, :, :, lanes].reshape(clss * PAD, piece)
            corr[...] += lax.dot_general(
                tmpl, images[comp, :, lanes], (((1,), (1,)), ((), ())),
                preferred_element_type=jnp.float32,
            )
            wide = tmpl.astype(jnp.float32)
            wide = wide * wide
            for q in range(piece // ANG):
                energy = energy + wide[:, q * ANG : (q + 1) * ANG]
            return energy
        return step

    energy = jnp.zeros((clss * PAD, ANG), jnp.float32)
    energy = lax.fori_loop(0, RAD * ANG // piece, correlate(pix), energy, unroll=True)
    for copy in forwards:
        copy.wait_recv()
    energy = lax.fori_loop(0, RAD * ANG // piece, correlate(other), energy, unroll=True)
    energy = jnp.sum(energy, axis=1, keepdims=True)

    turned = jnp.transpose(corr[...] - 0.5 * energy).reshape(ROT * shifts, count, clss * PAD)
    slot = lax.broadcasted_iota(jnp.int32, (count, clss * PAD), 1)
    inverse = 1.0 / noise
    size_block = CLASS_COUNT // clss
    real_class = lax.rem(slot, PAD) < size_block
    class_index = lax.div(slot, PAD) * size_block + lax.rem(slot, PAD)
    match = jnp.where(class_index == label, PRIOR_REWARD, 0.0)
    match = jnp.where(real_class, match, -1e30)
    values = []
    for rot in range(ROT):
        turn = lax.rem(rot + ROT - prior, ROT)
        level = jnp.where(turn == 0, KAPPA, jnp.where(turn == 2, -KAPPA, 0.0)) + match
        for t in range(shifts):
            x, y = move_ref[t, 0], move_ref[t, 1]
            move_prior = -MOVE_WEIGHT * (x * x + y * y).astype(jnp.float32)
            values.append(turned[rot * shifts + t] * inverse + (level + move_prior))
    highest = functools.reduce(jnp.maximum, values)
    highest = jnp.max(highest, axis=1, keepdims=True)
    summed = functools.reduce(jnp.add, [jnp.exp(v - highest) for v in values])
    evidence = highest + jnp.log(jnp.sum(summed, axis=1, keepdims=True))
    posterior = [
        jnp.exp(v - evidence).astype(jnp.bfloat16).astype(jnp.float32) for v in values
    ]
    weights = jnp.sum(functools.reduce(jnp.add, posterior), axis=0, keepdims=True)
    evidence_row = jnp.sum(evidence + jnp.zeros((count, clss * PAD), jnp.float32), axis=0, keepdims=True)
    first_row = lax.broadcasted_iota(jnp.int32, (8, clss * PAD), 0) == 0
    small_a[...] = jnp.where(first_row, weights, evidence_row)
    small_sib = send(small_a, small_in.at[0], small_s.at[0], small_r.at[0], sibling)
    posterior = jnp.transpose(jnp.concatenate(posterior, axis=0)).astype(jnp.bfloat16)

    def block_dot(d, half, comp):
        lanes = pl.ds(pl.multiple_of((d * 2 + half) * chunk, chunk), chunk)
        return jnp.dot(
            posterior, images[comp, :, lanes], preferred_element_type=jnp.float32
        ).reshape(clss, PAD, chunk)

    order = [lax.rem(dom + j + 1, doms) for j in range(doms)]
    sib_copies, cls_copies = [], []

    def finish(j):
        sib_copies[j].wait_recv()
        for comp in range(2):
            value = total[j, :, comp] + sib_in[j, :, comp].astype(jnp.float32)
            total[j, :, comp] = value
            cls_out[j, :, comp] = value.astype(jnp.bfloat16)
        cls_copies.append([
            send(cls_out.at[j, lax.rem(cls + k + 1, clss)], cls_in.at[j, k],
                 cls_s.at[j, k], cls_r.at[j, k], target)
            for k, target in enumerate(cls_peers)
        ])

    for j in range(doms):
        for comp in range(2):
            sib_out[j, :, comp] = block_dot(order[j], other, comp).astype(jnp.bfloat16)
        sib_copies.append(send(sib_out.at[j], sib_in.at[j], sib_s.at[j], sib_r.at[j], sibling))
        if j:
            finish(j - 1)
        for comp in range(2):
            total[j, :, comp] = block_dot(order[j], pix, comp)
        if j == 0:
            small_sib.wait_recv()
            small_b[...] = small_a[...] + small_in[0]
            small_cls = [
                send(small_b, small_in.at[1 + k], small_s.at[1 + k], small_r.at[1 + k], target)
                for k, target in enumerate(cls_peers)
            ]
    finish(doms - 1)

    for copy in small_cls:
        copy.wait_recv()
    small_c[...] = functools.reduce(jnp.add, [small_b[...]] + [small_in[1 + k] for k in range(clss - 1)])
    small_dom = [
        send(small_c, small_in.at[clss + k], small_s.at[clss + k], small_r.at[clss + k], target)
        for k, target in enumerate(dom_peers)
    ]

    dom_copies = []
    for j in range(doms):
        for copy in cls_copies[j]:
            copy.wait_recv()
        value = total[j, cls]
        for k in range(clss - 1):
            value = value + cls_in[j, k].astype(jnp.float32)
        if j < doms - 1:
            dom_out[j] = value.astype(jnp.bfloat16)
            dom_copies.append(
                send(dom_out.at[j], dom_in.at[j], dom_s.at[j], dom_r.at[j], dom_peers[j])
            )
    for j in range(doms - 1):
        small_dom[j].wait_recv()
    small = functools.reduce(
        jnp.add, [small_c[...]] + [small_in[clss + k] for k in range(doms - 1)]
    )
    own_weights = functools.reduce(
        jnp.add, [jnp.where(cls == k, small[0:1, k * PAD : (k + 1) * PAD], 0.0) for k in range(clss)]
    )
    weight_ref[...] = own_weights[:, :size_block]
    evidence_ref[...] = small[1:2, 0:1] * (1.0 / (count * doms * clss * 2))
    for j in range(doms - 1):
        dom_copies[j].wait_recv()
        value = value + dom_in[j].astype(jnp.float32)
    out_ref[...] = value
    for copy in gathers + pairs + forwards + sib_copies + sum(cls_copies, []) + dom_copies:
        copy.wait_send()
    for copy in [small_sib] + small_cls + small_dom:
        copy.wait_send()


def fused_body(doms, clss, particles, templates, offsets, micrograph, noise_var, prior_rot, earlier_class_labels):
    count, size_block, shifts = particles.shape[0], templates.shape[0], offsets.shape[0]
    chunk = RAD * ANG // (doms * 2)
    tmpl = jnp.pad(jnp.transpose(templates, (1, 0, 2)), ((0, 0), (0, PAD - size_block), (0, 0)))
    rows = ROT * shifts * count
    bf, f32 = jnp.bfloat16, jnp.float32
    dma = pltpu.SemaphoreType.DMA
    vmem = pl.BlockSpec(memory_space=pltpu.VMEM)
    smem = pl.BlockSpec(memory_space=pltpu.SMEM)
    sums, weights, evidence = pl.pallas_call(
        functools.partial(fused, (doms, clss, count, shifts, chunk)),
        out_shape=[
            jax.ShapeDtypeStruct((2, PAD, chunk), f32),
            jax.ShapeDtypeStruct((1, size_block), f32),
            jax.ShapeDtypeStruct((1, 1), f32),
        ],
        in_specs=[pl.BlockSpec(memory_space=pl.ANY), vmem, vmem] + [smem] * 5,
        out_specs=[vmem] * 3,
        scratch_shapes=[
            pltpu.VMEM(particles.shape, f32),
            pltpu.VMEM((2, clss, PAD, RAD * ANG), bf),
            pltpu.VMEM((2, rows, RAD * ANG), bf),
            pltpu.VMEM((clss * PAD, rows), f32),
            pltpu.VMEM((doms, clss, 2, PAD, chunk), f32),
            pltpu.VMEM((doms, clss, 2, PAD, chunk), bf),
            pltpu.VMEM((doms, clss, 2, PAD, chunk), bf),
            pltpu.VMEM((doms, clss, 2, PAD, chunk), bf),
            pltpu.VMEM((doms, clss - 1, 2, PAD, chunk), bf),
            pltpu.VMEM((doms - 1, 2, PAD, chunk), bf),
            pltpu.VMEM((doms - 1, 2, PAD, chunk), bf),
            pltpu.VMEM((clss + doms - 1, 8, clss * PAD), f32),
            dma((2,)), dma, dma((2, clss - 1)), dma((2, clss - 1)), dma((3, clss - 1)), dma((3, clss - 1)),
            dma((doms,)), dma((doms,)), dma((doms, clss - 1)), dma((doms, clss - 1)),
            dma((doms - 1,)), dma((doms - 1,)), dma((clss + doms - 1,)), dma((clss + doms - 1,)),
            pltpu.VMEM((8, clss * PAD), f32),
            pltpu.VMEM((8, clss * PAD), f32),
            pltpu.VMEM((8, clss * PAD), f32),
            dma((clss - 1,)), dma((clss - 1,)),
        ],
        compiler_params=pltpu.CompilerParams(
            collective_id=0, has_side_effects=True, vmem_limit_bytes=44 * 2**20
        ),
    )(
        particles, tmpl, jnp.asarray(wave_tables()),
        micrograph, noise_var, prior_rot, earlier_class_labels, offsets,
    )
    class_sums = jnp.transpose(sums[:, :size_block], (1, 0, 2))
    return class_sums, weights.reshape(size_block), evidence.reshape(1)


def solution(mesh):
    in_specs = (
        P(("groups", "dom", "cls", "pix"), None, None),
        P(("groups", "cls"), None, None),
        P(),
        P(("groups", "dom", "cls", "pix")),
        P("groups"),
        P(("groups", "dom", "cls", "pix")),
        P(("groups", "dom", "cls", "pix")),
    )
    out_specs = (P(("groups", "cls"), None, ("dom", "pix")), P(("groups", "cls")), P("groups"))
    doms, clss = mesh.shape["dom"], mesh.shape["cls"]
    whole_radii = RAD % (doms * mesh.shape["pix"]) == 0
    fits = mesh.shape["pix"] == 2 and doms % 2 == 0 and clss > 1 and clss * PAD == ANG
    chosen = functools.partial(fused_body, doms, clss) if whole_radii and fits else body
    return jax.shard_map(chosen, mesh=mesh, in_specs=in_specs, out_specs=out_specs, check_vma=False)
```

```python
import functools
import math

import jax
import jax.numpy as jnp
import numpy as np
from jax import lax
from jax.experimental import pallas as pl
from jax.experimental.pallas import tpu as pltpu
from jax.sharding import PartitionSpec as P

RAD = 32
ANG = 128
CLASS_COUNT = 100
ROT = 4


KAPPA = 2.0
PRIOR_REWARD = 1.5
MOVE_WEIGHT = 0.125


def shifted_images(particles, offsets):
    radius = jnp.arange(RAD, dtype=jnp.float32) + 1.0
    angle_grid = 2.0 * math.pi / ANG * jnp.arange(ANG, dtype=jnp.float32)
    wave_first = (radius[:, None] * jnp.cos(angle_grid)[None, :]).reshape(-1)
    wave_second = (radius[:, None] * jnp.sin(angle_grid)[None, :]).reshape(-1)
    offset_first = offsets[:, 0].astype(jnp.float32)
    offset_second = offsets[:, 1].astype(jnp.float32)
    phase_table = (
        2.0
        * math.pi
        / (2 * RAD)
        * (
            offset_first[:, None] * wave_first[None, :]
            + offset_second[:, None] * wave_second[None, :]
        )
    )
    cosine = jnp.cos(phase_table)[None]
    sine_part = jnp.sin(phase_table)[None]
    real_part = particles[:, 0, :][:, None, :]
    imag_part = particles[:, 1, :][:, None, :]
    new_real = real_part * cosine + imag_part * sine_part
    new_imag = imag_part * cosine - real_part * sine_part
    return jnp.stack([new_real, new_imag], axis=2).astype(jnp.bfloat16)


def row_terms(micrograph, prior_rot, earlier_class_labels, noise_var, offsets):
    inverse = jnp.sum(
        jnp.where(
            micrograph[:, None] == jnp.arange(noise_var.shape[0], dtype=jnp.int32)[None, :],
            1.0 / noise_var[None, :],
            0.0,
        ),
        axis=1,
    )
    turn_prior = KAPPA * jnp.cos(
        2.0
        * math.pi
        / ROT
        * (jnp.arange(ROT, dtype=jnp.int32)[:, None] - prior_rot[None, :]).astype(jnp.float32)
    )
    class_agreement = jnp.where(
        jnp.arange(CLASS_COUNT, dtype=jnp.int32)[:, None] == earlier_class_labels[None, :],
        PRIOR_REWARD,
        0.0,
    )
    offset_first = offsets[:, 0].astype(jnp.float32)
    offset_second = offsets[:, 1].astype(jnp.float32)
    move_prior = -MOVE_WEIGHT * (offset_first * offset_first + offset_second * offset_second)
    return (inverse, turn_prior, class_agreement, move_prior)


def rotate_block(block_tmpl, first_rot, group_size):
    size_block = block_tmpl.shape[0]
    polar_grid = block_tmpl.reshape(size_block, 2, RAD, ANG)
    doubled = jnp.concatenate([polar_grid, polar_grid], axis=3)
    step_size = ANG // ROT
    pieces = [
        lax.dynamic_slice_in_dim(doubled, ANG - (first_rot + within) * step_size, ANG, 3)
        for within in range(group_size)
    ]
    return jnp.stack(pieces, axis=0).reshape(group_size * size_block, 2 * RAD * ANG)


def block_energy(block_tmpl):
    widened = block_tmpl.astype(jnp.float32)
    return jnp.sum(widened * widened, axis=(1, 2))


def split_features(sum_store):
    return lax.psum_scatter(sum_store, ("dom", "pix"), scatter_dimension=2, tiled=True)


def body(particles, templates, offsets, micrograph, noise_var, prior_rot, earlier_class_labels):
    particle_count = particles.shape[0]
    size_block = templates.shape[0]
    shift_count = offsets.shape[0]
    cls_size = lax.axis_size("cls")
    cls_index = lax.axis_index("cls")
    total_particles = particle_count * lax.axis_size("dom") * cls_size * lax.axis_size("pix")
    group_size = math.gcd(ROT, 4)
    group_count = ROT // group_size
    step_size = ANG // ROT
    feature_count = RAD * ANG
    kept_shape = (group_count, group_size, size_block, particle_count, shift_count)

    def scores(block_tmpl, energy, first_class, first_rot, images_flat, row_extras):
        inverse, turn_prior, class_agreement, move_prior = row_extras
        rotated = rotate_block(block_tmpl, first_rot, group_size)
        correlation = lax.dot_general(
            rotated, images_flat, (((1,), (1,)), ((), ())), preferred_element_type=jnp.float32
        )
        correlation = correlation.reshape(group_size, size_block, particle_count, shift_count)
        match_part = lax.dynamic_slice_in_dim(class_agreement, first_class, size_block, 0)
        return (
            (correlation - 0.5 * energy[None, :, None, None]) * inverse[None, None, :, None]
            + move_prior[None, None, None, :]
            + turn_prior[:, None, :, None]
            + match_part[None, :, :, None]
        )

    def normalize_block(block_tmpl, first_class, images_flat, row_extras, loop_state):
        energy = block_energy(block_tmpl)

        def normalize_group_turn(group_index, inner_state):
            highest, running_sum, kept = inner_state
            values = scores(
                block_tmpl, energy, first_class, group_index * group_size, images_flat, row_extras
            )
            new_high = jnp.maximum(highest, jnp.max(values, axis=(0, 1, 3)))
            running_sum = running_sum * jnp.exp(highest - new_high) + jnp.sum(
                jnp.exp(values - new_high[None, None, :, None]), axis=(0, 1, 3)
            )
            kept = lax.dynamic_update_index_in_dim(kept, values, group_index, 0)
            return (new_high, running_sum, kept)

        initial = (loop_state[0], loop_state[1], jnp.zeros(kept_shape, jnp.float32))
        return lax.fori_loop(0, group_count, normalize_group_turn, initial)

    def collect_block(kept, images_flat, evidence):

        def collect_group_turn(group_index, inner_state):
            block_sum, block_weight = inner_state
            first_rot = group_index * group_size
            values = lax.dynamic_index_in_dim(kept, group_index, 0, keepdims=False)
            posterior = jnp.exp(values - evidence[None, None, :, None]).astype(jnp.bfloat16)
            block_weight = block_weight + jnp.sum(posterior.astype(jnp.float32), axis=(0, 2, 3))
            aligned = jnp.dot(
                posterior.reshape(group_size * size_block, particle_count * shift_count),
                images_flat,
                preferred_element_type=jnp.float32,
            )
            aligned = aligned.reshape(group_size, size_block, 2, RAD, ANG)
            doubled = jnp.concatenate([aligned, aligned], axis=4)
            for within in range(group_size):
                block_sum = block_sum + lax.dynamic_slice_in_dim(
                    doubled[within], (first_rot + within) * step_size, ANG, 3
                )
            return (block_sum, block_weight)

        initial = (
            jnp.zeros((size_block, 2, RAD, ANG), jnp.float32),
            jnp.zeros((size_block,), jnp.float32),
        )
        block_sum, block_weight = lax.fori_loop(0, group_count, collect_group_turn, initial)
        return (block_sum.reshape(size_block, 2, feature_count), block_weight)

    own_first = cls_index * size_block
    all_kept = jnp.zeros((cls_size,) + kept_shape, jnp.float32)
    prepare_images_flat = shifted_images(particles, offsets).reshape(
        particles.shape[0] * shift_count, 2 * feature_count
    )
    prepare_row_extras = row_terms(micrograph, prior_rot, earlier_class_labels, noise_var, offsets)
    images_flat = prepare_images_flat
    row_extras = prepare_row_extras
    held_block = lax.all_gather(templates, "cls", axis=0, tiled=True)

    def current_block(held_now, owner_index):
        return lax.dynamic_slice_in_dim(held_now, owner_index * size_block, size_block, 0)

    def first_turn(turn_index, outer_state):
        held_now, highest, running_sum, retained_entries = outer_state
        owner_index = (cls_index - turn_index) % cls_size
        highest, running_sum, kept = normalize_block(
            current_block(held_now, owner_index),
            owner_index * size_block,
            images_flat,
            row_extras,
            (highest, running_sum),
        )
        retained_entries = lax.dynamic_update_index_in_dim(retained_entries, kept, turn_index, 0)
        return (held_now, highest, running_sum, retained_entries)

    highest, running_sum = (
        jnp.full((particle_count,), -jnp.inf, jnp.float32),
        jnp.zeros((particle_count,), jnp.float32),
    )
    held_block, highest, running_sum, all_kept = lax.fori_loop(
        0, cls_size, first_turn, (held_block, highest, running_sum, all_kept)
    )
    evidence = highest + jnp.log(running_sum)

    def second_turn(turn_index, outer_state):
        sum_store, weights_all = outer_state
        owner_index = (cls_index - turn_index) % cls_size
        kept = lax.dynamic_index_in_dim(all_kept, turn_index, 0, keepdims=False)
        block_sum, block_weight = collect_block(kept, images_flat, evidence)
        weights_all = lax.dynamic_update_slice_in_dim(
            weights_all, block_weight, owner_index * size_block, 0
        )
        sum_store = lax.dynamic_update_slice_in_dim(
            sum_store, block_sum, owner_index * size_block, 0
        )
        return (sum_store, weights_all)

    store_rows = CLASS_COUNT
    initial = (
        jnp.zeros((store_rows, 2, feature_count), jnp.float32),
        jnp.zeros((CLASS_COUNT,), jnp.float32),
    )
    sum_store, weights_all = lax.fori_loop(0, cls_size, second_turn, initial)
    local_evidence = jnp.sum(evidence)
    sum_store = lax.psum_scatter(sum_store, "cls", scatter_dimension=0, tiled=True)
    class_sums = split_features(sum_store)
    weight_total, summed_evidence = lax.psum(
        (weights_all, local_evidence[None]), ("dom", "cls", "pix")
    )
    class_weights = lax.dynamic_slice_in_dim(weight_total, own_first, size_block, 0)
    log_evidence = summed_evidence / total_particles
    return (class_sums, class_weights, log_evidence)


AXES = ("groups", "dom", "cls", "pix")
PAD = 32


def wave_tables():
    radius = np.arange(RAD) + 1.0
    angle = 2.0 * np.pi / ANG * np.arange(ANG)
    first = (radius[:, None] * np.cos(angle)[None, :]).reshape(-1) * (2.0 * np.pi / (2 * RAD))
    second = (radius[:, None] * np.sin(angle)[None, :]).reshape(-1) * (2.0 * np.pi / (2 * RAD))
    rows = [np.cos(first), np.sin(first), np.cos(second), np.sin(second)]
    return np.stack(rows + rows).astype(np.float32)


def powers(cosine, sine_part, amount):
    c2, s2 = cosine * cosine - sine_part * sine_part, 2.0 * cosine * sine_part
    c3, s3 = c2 * cosine - s2 * sine_part, s2 * cosine + c2 * sine_part
    size = jnp.abs(amount)
    c = jnp.where(size < 0.5, 1.0, jnp.where(size < 1.5, cosine, jnp.where(size < 2.5, c2, c3)))
    s = jnp.where(size < 0.5, 0.0, jnp.where(size < 1.5, sine_part, jnp.where(size < 2.5, s2, s3)))
    return c, jnp.where(amount < 0.0, -s, s)


def fused(
    dims, part_hbm, tmpl_ref, wave_ref, micro_ref, noise_ref, prior_ref, label_ref, move_ref,
    out_ref, weight_ref, evidence_ref, part_ref, held, images, corr, total, sib_out, sib_in, cls_out, cls_in, dom_out, dom_in, small_in,
    own_sem, part_sem, gather_s, gather_r, forward_s, forward_r, sib_s, sib_r, cls_s, cls_r,
    dom_s, dom_r, small_s, small_r, small_a, small_b, small_c, pair_s, pair_r,
):
    doms, clss, count, shifts, chunk = dims
    group, dom = lax.axis_index("groups"), lax.axis_index("dom")
    cls, pix = lax.axis_index("cls"), lax.axis_index("pix")
    other = 1 - pix
    sibling = (group, dom, cls, other)
    cls_peers = [(group, dom, lax.rem(cls + k, clss), pix) for k in range(1, clss)]
    dom_peers = [(group, lax.rem(dom + k, doms), cls, pix) for k in range(1, doms)]
    mesh_id = pl.DeviceIdType.MESH

    def send(src, dst, s, r, target):
        copy = pltpu.make_async_remote_copy(
            src_ref=src, dst_ref=dst, send_sem=s, recv_sem=r,
            device_id=target, device_id_type=mesh_id,
        )
        copy.start()
        return copy

    barrier = pltpu.get_barrier_semaphore()
    for target in [sibling] + cls_peers + dom_peers:
        pl.semaphore_signal(barrier, inc=1, device_id=target, device_id_type=mesh_id)
    pl.semaphore_wait(barrier, clss + doms - 1)

    odd = lax.rem(dom, 2)
    partner = (group, dom + 1 - 2 * odd, cls, pix)
    features = RAD * ANG
    part_size, common = features // 8, 3 * features // 4
    own_lanes = pl.ds(pl.multiple_of(odd * part_size, ANG), part_size)
    pair_lanes = pl.ds(pl.multiple_of((1 - odd) * part_size, ANG), part_size)
    common_lanes = pl.ds(2 * part_size, common)
    gathers = []
    for n, lanes in enumerate((own_lanes, common_lanes)):
        for k, target in enumerate(cls_peers):
            gathers.append(
                send(tmpl_ref.at[pix, :, lanes], held.at[pix, cls, :, lanes],
                     gather_s.at[n, k], gather_r.at[n, k], target)
            )
    own_copies = [
        pltpu.make_async_copy(tmpl_ref.at[c], held.at[c, cls], own_sem.at[c]) for c in range(2)
    ]
    part_copy = pltpu.make_async_copy(part_hbm, part_ref, part_sem)
    part_copy.start()
    for copy in own_copies:
        copy.start()

    rows = lax.broadcasted_iota(jnp.int32, (count, ANG), 0)
    noise = jnp.ones((count, ANG), jnp.float32)
    prior = jnp.zeros((count, ANG), jnp.int32)
    label = jnp.zeros((count, ANG), jnp.int32)
    for i in range(count):
        noise = jnp.where(rows == i, noise_ref[micro_ref[i]], noise)
        prior = jnp.where(rows == i, prior_ref[i], prior)
        label = jnp.where(rows == i, label_ref[i], label)
    move_x = jnp.zeros((count, ANG), jnp.int32)
    move_y = jnp.zeros((count, ANG), jnp.int32)
    for t in range(shifts):
        move_x = jnp.where(rows == t, move_ref[t, 0], move_x)
        move_y = jnp.where(rows == t, move_ref[t, 1], move_y)
    move_x, move_y = move_x.astype(jnp.float32), move_y.astype(jnp.float32)
    part_copy.wait()

    step_size = ANG // ROT
    per_rot = shifts * count

    def make_images(g, carry):
        lanes = pl.ds(pl.multiple_of(g * ANG, ANG), ANG)
        waves = wave_ref[:, lanes]
        cx, sx = powers(waves[0:1], waves[1:2], move_x)
        cy, sy = powers(waves[2:3], waves[3:4], move_y)
        cosine = cx * cy - sx * sy
        sine_part = sx * cy + cx * sy
        real, imag = part_ref[:, 0, lanes], part_ref[:, 1, lanes]
        for rot in range(ROT):
            if rot:
                turn = ANG - rot * step_size
                co, si = pltpu.roll(cosine, turn, 1), pltpu.roll(sine_part, turn, 1)
                re, im = pltpu.roll(real, turn, 1), pltpu.roll(imag, turn, 1)
            else:
                co, si, re, im = cosine, sine_part, real, imag
            for t in range(shifts):
                c, s = co[t : t + 1], si[t : t + 1]
                row = rot * per_rot + t * count
                images[0, row : row + count, lanes] = (re * c + im * s).astype(jnp.bfloat16)
                images[1, row : row + count, lanes] = (im * c - re * s).astype(jnp.bfloat16)
        return carry

    lax.fori_loop(0, RAD, make_images, 0)

    owners = [lax.rem(cls + clss - 1 - k, clss) for k in range(clss - 1)]
    forwards, pairs = [], []

    def forward(n, k, lanes):
        block = held.at[pix, owners[k], :, lanes]
        forwards.append(send(block, block, forward_s.at[n, k], forward_r.at[n, k], sibling))

    for k in range(clss - 1):
        gathers[k].wait_recv()
        block = held.at[pix, owners[k], :, own_lanes]
        pairs.append(send(block, block, pair_s.at[k], pair_r.at[k], partner))
        forward(0, k, own_lanes)
    for k in range(clss - 1):
        gathers[clss - 1 + k].wait_recv()
        forward(1, k, common_lanes)
    for k in range(clss - 1):
        pairs[k].wait_recv()
        forward(2, k, pair_lanes)
    for copy in own_copies:
        copy.wait()

    piece = 512
    corr[...] = jnp.zeros_like(corr)

    def correlate(comp):
        def step(n, energy):
            lanes = pl.ds(pl.multiple_of(n * piece, piece), piece)
            tmpl = held[comp, :, :, lanes].reshape(clss * PAD, piece)
            corr[...] += lax.dot_general(
                tmpl, images[comp, :, lanes], (((1,), (1,)), ((), ())),
                preferred_element_type=jnp.float32,
            )
            wide = tmpl.astype(jnp.float32)
            wide = wide * wide
            for q in range(piece // ANG):
                energy = energy + wide[:, q * ANG : (q + 1) * ANG]
            return energy
        return step

    energy = jnp.zeros((clss * PAD, ANG), jnp.float32)
    energy = lax.fori_loop(0, RAD * ANG // piece, correlate(pix), energy, unroll=True)
    for copy in forwards:
        copy.wait_recv()
    energy = lax.fori_loop(0, RAD * ANG // piece, correlate(other), energy, unroll=True)
    energy = jnp.sum(energy, axis=1, keepdims=True)

    turned = jnp.transpose(corr[...] - 0.5 * energy).reshape(ROT * shifts, count, clss * PAD)
    slot = lax.broadcasted_iota(jnp.int32, (count, clss * PAD), 1)
    inverse = 1.0 / noise
    size_block = CLASS_COUNT // clss
    real_class = lax.rem(slot, PAD) < size_block
    class_index = lax.div(slot, PAD) * size_block + lax.rem(slot, PAD)
    match = jnp.where(class_index == label, PRIOR_REWARD, 0.0)
    match = jnp.where(real_class, match, -1e30)
    values = []
    for rot in range(ROT):
        turn = lax.rem(rot + ROT - prior, ROT)
        level = jnp.where(turn == 0, KAPPA, jnp.where(turn == 2, -KAPPA, 0.0)) + match
        for t in range(shifts):
            x, y = move_ref[t, 0], move_ref[t, 1]
            move_prior = -MOVE_WEIGHT * (x * x + y * y).astype(jnp.float32)
            values.append(turned[rot * shifts + t] * inverse + (level + move_prior))
    highest = functools.reduce(jnp.maximum, values)
    highest = jnp.max(highest, axis=1, keepdims=True)
    summed = functools.reduce(jnp.add, [jnp.exp(v - highest) for v in values])
    evidence = highest + jnp.log(jnp.sum(summed, axis=1, keepdims=True))
    posterior = [
        jnp.exp(v - evidence).astype(jnp.bfloat16).astype(jnp.float32) for v in values
    ]
    weights = jnp.sum(functools.reduce(jnp.add, posterior), axis=0, keepdims=True)
    evidence_row = jnp.sum(evidence + jnp.zeros((count, clss * PAD), jnp.float32), axis=0, keepdims=True)
    first_row = lax.broadcasted_iota(jnp.int32, (8, clss * PAD), 0) == 0
    small_a[...] = jnp.where(first_row, weights, evidence_row)
    small_sib = send(small_a, small_in.at[0], small_s.at[0], small_r.at[0], sibling)
    posterior = jnp.transpose(jnp.concatenate(posterior, axis=0)).astype(jnp.bfloat16)

    def block_dot(d, half, comp):
        lanes = pl.ds(pl.multiple_of((d * 2 + half) * chunk, chunk), chunk)
        return jnp.dot(
            posterior, images[comp, :, lanes], preferred_element_type=jnp.float32
        ).reshape(clss, PAD, chunk)

    order = [lax.rem(dom + j + 1, doms) for j in range(doms)]
    sib_copies, cls_copies = [], []

    def finish(j):
        sib_copies[j].wait_recv()
        for comp in range(2):
            value = total[j, :, comp] + sib_in[j, :, comp].astype(jnp.float32)
            total[j, :, comp] = value
            cls_out[j, :, comp] = value.astype(jnp.bfloat16)
        cls_copies.append([
            send(cls_out.at[j, lax.rem(cls + k + 1, clss)], cls_in.at[j, k],
                 cls_s.at[j, k], cls_r.at[j, k], target)
            for k, target in enumerate(cls_peers)
        ])

    for j in range(doms):
        for comp in range(2):
            sib_out[j, :, comp] = block_dot(order[j], other, comp).astype(jnp.bfloat16)
        sib_copies.append(send(sib_out.at[j], sib_in.at[j], sib_s.at[j], sib_r.at[j], sibling))
        if j:
            finish(j - 1)
        for comp in range(2):
            total[j, :, comp] = block_dot(order[j], pix, comp)
        if j == 0:
            small_sib.wait_recv()
            small_b[...] = small_a[...] + small_in[0]
            small_cls = [
                send(small_b, small_in.at[1 + k], small_s.at[1 + k], small_r.at[1 + k], target)
                for k, target in enumerate(cls_peers)
            ]
    finish(doms - 1)

    for copy in small_cls:
        copy.wait_recv()
    small_c[...] = functools.reduce(jnp.add, [small_b[...]] + [small_in[1 + k] for k in range(clss - 1)])
    small_dom = [
        send(small_c, small_in.at[clss + k], small_s.at[clss + k], small_r.at[clss + k], target)
        for k, target in enumerate(dom_peers)
    ]

    dom_copies = []
    for j in range(doms):
        for copy in cls_copies[j]:
            copy.wait_recv()
        value = total[j, cls]
        for k in range(clss - 1):
            value = value + cls_in[j, k].astype(jnp.float32)
        if j < doms - 1:
            dom_out[j] = value.astype(jnp.bfloat16)
            dom_copies.append(
                send(dom_out.at[j], dom_in.at[j], dom_s.at[j], dom_r.at[j], dom_peers[j])
            )
    for j in range(doms - 1):
        small_dom[j].wait_recv()
    small = functools.reduce(
        jnp.add, [small_c[...]] + [small_in[clss + k] for k in range(doms - 1)]
    )
    own_weights = functools.reduce(
        jnp.add, [jnp.where(cls == k, small[0:1, k * PAD : (k + 1) * PAD], 0.0) for k in range(clss)]
    )
    weight_ref[...] = own_weights[:, :size_block]
    evidence_ref[...] = small[1:2, 0:1] * (1.0 / (count * doms * clss * 2))
    for j in range(doms - 1):
        dom_copies[j].wait_recv()
        value = value + dom_in[j].astype(jnp.float32)
    out_ref[...] = value
    for copy in gathers + pairs + forwards + sib_copies + sum(cls_copies, []) + dom_copies:
        copy.wait_send()
    for copy in [small_sib] + small_cls + small_dom:
        copy.wait_send()


def fused_body(doms, clss, particles, templates, offsets, micrograph, noise_var, prior_rot, earlier_class_labels):
    count, size_block, shifts = particles.shape[0], templates.shape[0], offsets.shape[0]
    chunk = RAD * ANG // (doms * 2)
    tmpl = jnp.pad(jnp.transpose(templates, (1, 0, 2)), ((0, 0), (0, PAD - size_block), (0, 0)))
    rows = ROT * shifts * count
    bf, f32 = jnp.bfloat16, jnp.float32
    dma = pltpu.SemaphoreType.DMA
    vmem = pl.BlockSpec(memory_space=pltpu.VMEM)
    smem = pl.BlockSpec(memory_space=pltpu.SMEM)
    sums, weights, evidence = pl.pallas_call(
        functools.partial(fused, (doms, clss, count, shifts, chunk)),
        out_shape=[
            jax.ShapeDtypeStruct((2, PAD, chunk), f32),
            jax.ShapeDtypeStruct((1, size_block), f32),
            jax.ShapeDtypeStruct((1, 1), f32),
        ],
        in_specs=[pl.BlockSpec(memory_space=pl.ANY), vmem, vmem] + [smem] * 5,
        out_specs=[vmem] * 3,
        scratch_shapes=[
            pltpu.VMEM(particles.shape, f32),
            pltpu.VMEM((2, clss, PAD, RAD * ANG), bf),
            pltpu.VMEM((2, rows, RAD * ANG), bf),
            pltpu.VMEM((clss * PAD, rows), f32),
            pltpu.VMEM((doms, clss, 2, PAD, chunk), f32),
            pltpu.VMEM((doms, clss, 2, PAD, chunk), bf),
            pltpu.VMEM((doms, clss, 2, PAD, chunk), bf),
            pltpu.VMEM((doms, clss, 2, PAD, chunk), bf),
            pltpu.VMEM((doms, clss - 1, 2, PAD, chunk), bf),
            pltpu.VMEM((doms - 1, 2, PAD, chunk), bf),
            pltpu.VMEM((doms - 1, 2, PAD, chunk), bf),
            pltpu.VMEM((clss + doms - 1, 8, clss * PAD), f32),
            dma((2,)), dma, dma((2, clss - 1)), dma((2, clss - 1)), dma((3, clss - 1)), dma((3, clss - 1)),
            dma((doms,)), dma((doms,)), dma((doms, clss - 1)), dma((doms, clss - 1)),
            dma((doms - 1,)), dma((doms - 1,)), dma((clss + doms - 1,)), dma((clss + doms - 1,)),
            pltpu.VMEM((8, clss * PAD), f32),
            pltpu.VMEM((8, clss * PAD), f32),
            pltpu.VMEM((8, clss * PAD), f32),
            dma((clss - 1,)), dma((clss - 1,)),
        ],
        compiler_params=pltpu.CompilerParams(
            collective_id=0, has_side_effects=True, vmem_limit_bytes=44 * 2**20
        ),
    )(
        particles, tmpl, jnp.asarray(wave_tables()),
        micrograph, noise_var, prior_rot, earlier_class_labels, offsets,
    )
    class_sums = jnp.transpose(sums[:, :size_block], (1, 0, 2))
    return class_sums, weights.reshape(size_block), evidence.reshape(1)


def solution(mesh):
    in_specs = (
        P(("groups", "dom", "cls", "pix"), None, None),
        P(("groups", "cls"), None, None),
        P(),
        P(("groups", "dom", "cls", "pix")),
        P("groups"),
        P(("groups", "dom", "cls", "pix")),
        P(("groups", "dom", "cls", "pix")),
    )
    out_specs = (P(("groups", "cls"), None, ("dom", "pix")), P(("groups", "cls")), P("groups"))
    doms, clss = mesh.shape["dom"], mesh.shape["cls"]
    whole_radii = RAD % (doms * mesh.shape["pix"]) == 0
    fits = mesh.shape["pix"] == 2 and doms % 2 == 0 and clss > 1 and clss * PAD == ANG
    chosen = functools.partial(fused_body, doms, clss) if whole_radii and fits else body
    return jax.shard_map(chosen, mesh=mesh, in_specs=in_specs, out_specs=out_specs, check_vma=False)
```
